32 devices in a mesh: box: 8 (over y, x, core), slab: 4 (over z).
Axes of the slice: x: 2, y: 2, z: 4, core: 2. Of those that a mesh axis runs over, the one named last changes fastest.
Arguments:
- velocity: bfloat16 [8, 3, 8, 16, 64, 128], P('box', None, None, None, 'slab'), may hold values from -6 to 6
- field: float32 [8, 3, 8, 16, 64], P('box', None, None, None, 'slab'), may hold values from -6 to 6
- conductivity: float32 [8, 8, 16, 64], P('box', None, None, 'slab'), may hold values from 0.5 to 2
- wall_flags: int32 [8, 8, 16, 64], P('box', None, None, 'slab'), may hold values 0 or 1
- leaf_solution: bfloat16 [8, 4, 512, 2048], P('box', 'slab'), may hold values from -0.125 to 0.125
- leaf_dtn: float32 [8, 4, 512, 512], P('box', 'slab'), as said below
Outputs:
- interface_two: float32 [8, 4, 256, 128], P('box', 'slab')
- neumann_two: float32 [8, 4, 512, 128], P('box', 'slab')
The draws below stay inside these ranges and needn't reach their ends.
Inputs may be any that keep to these rules, and one draw needn't show every extreme that they name: `leaf_dtn`: every leaf map is symmetric positive definite.
All inputs are finite; a program needn't handle non-finite values. No bound on the sum of `wall_flags` on one device may be relied on, other than what follows from the above.
Results may differ from the reference program's by a relative error of at most 0.0029.
Values sent between devices are 32-bit elements; how exact they have to be, the bound alone decides.
A program may use at most 64 MiB of HBM per device.

```python
import math
import jax
import jax.numpy as jnp
from jax import lax

LX = 8
LY = 16
R = 128
BOXES = 8
SLABS = 4
NZ = 64
FACE = 256
CELLS = 2048


DIAGONAL_SHIFT = 0.5


def draw_leaf_dtn(key, part):
    key_base = jax.random.fold_in(jax.random.fold_in(key, 7), 0)
    order = 2 * FACE
    shape = (BOXES, SLABS, order, order)
    factor = jax.random.normal(key_base, shape, jnp.float32)

    def gram(block):
        return jnp.einsum('sik,sjk->sij', block, block, precision=lax.Precision.HIGHEST)
    product = lax.map(gram, factor) * (1.0 / order)
    rows = jnp.arange(order, dtype=jnp.int32)
    identity = (rows[:, None] == rows[None, :]).astype(jnp.float32)
    result = product + DIAGONAL_SHIFT * identity
    return result


def with_ends(drawn, stream_key, smallest, top_value):
    index_at = [jax.random.randint(jax.random.fold_in(stream_key, axis), (), 0, length) for axis, length in enumerate(drawn.shape)]
    longest = drawn.shape.index(max(drawn.shape))
    next_to = index_at[:longest] + [(index_at[longest] + 1) % drawn.shape[longest]] + index_at[longest + 1:]
    return drawn.at[tuple(index_at)].set(smallest).at[tuple(next_to)].set(top_value)


def shard_levels(stream_key, dims, shards, low, largest):
    gain = 1.0
    for axis_at, parts in shards:
        steps = jax.random.uniform(jax.random.fold_in(jax.random.fold_in(stream_key, 6), axis_at), (parts,), jnp.float32, low / len(shards), largest / len(shards))
        gain = gain * jnp.repeat(jnp.exp(steps), dims[axis_at] // parts).reshape((-1,) + (1,) * (len(dims) - 1 - axis_at))
    return gain


def noise(stream_key, extent, deviation, bound, cuts=(), kind=jnp.bfloat16):
    gain = shard_levels(stream_key, extent, cuts, -0.22, 0.18) if cuts else 1.0
    entries = jax.random.normal(stream_key, extent, jnp.float32) * deviation * gain
    return jnp.minimum(jnp.maximum(entries, -bound), bound).astype(kind)


def setup_inputs(seed: int = 0) -> dict:
    seeds = jax.random.split(jax.random.key(seed), 7)
    return {
        "velocity": noise(seeds[0], (BOXES, 3, LX, LY, NZ, R), 1.0, 6.0, ((0, 8), (4, 4))),
        "field": noise(seeds[1], (BOXES, 3, LX, LY, NZ), 1.0, 6.0, ((0, 8), (4, 4)), jnp.float32),
        "conductivity": jnp.clip(jnp.exp(math.log(2.0) - 1.3862944 * jax.random.uniform(seeds[2], (BOXES, LX, LY, NZ), jnp.float32) ** shard_levels(seeds[2], (BOXES, LX, LY, NZ), ((0, 8), (3, 4)), -0.2, 0.2)), 0.5, 2.0),
        "wall_flags": with_ends((jax.random.randint(seeds[3], (BOXES, LX, LY, NZ), 0, 4) < 1).astype(jnp.int32), jax.random.fold_in(seeds[3], 1), 0, 1),
        "leaf_solution": noise(seeds[4], (BOXES, SLABS, 2 * FACE, CELLS), CELLS ** -0.5, 0.125, ((0, 8), (1, 4))),
        "leaf_dtn": draw_leaf_dtn(jax.random.fold_in(seeds[6], 71), 0),
    }


WALL_RATIO = 8.0
HIGHEST = lax.Precision.HIGHEST

def currents(velocity, field, conductivity, wall_flags):
    sigma = conductivity * jnp.where(wall_flags == 1, WALL_RATIO, 1.0).astype(conductivity.dtype)
    speed = velocity.astype(jnp.float32)
    magnet = field[..., None]
    weight = sigma[..., None]
    elec_x = speed[1] * magnet[2] - speed[2] * magnet[1]
    elec_y = speed[2] * magnet[0] - speed[0] * magnet[2]
    elec_z = speed[0] * magnet[1] - speed[1] * magnet[0]
    return (weight * elec_x, weight * elec_y, weight * elec_z)

def divergence(flow_x, flow_y, padded_z):
    padded_x = jnp.pad(flow_x, ((1, 1), (0, 0), (0, 0), (0, 0)))
    padded_y = jnp.pad(flow_y, ((0, 0), (1, 1), (0, 0), (0, 0)))
    return 0.5 * (padded_x[2:] - padded_x[:-2] + (padded_y[:, 2:] - padded_y[:, :-2]) + (padded_z[:, :, 2:] - padded_z[:, :, :-2]))

def merge(left_map, left_data, right_map, right_data, need_map):
    width = left_map.shape[0] // 2
    schur = left_map[width:, width:] + right_map[:width, :width]
    coupling = jnp.concatenate([left_map[width:, :width], right_map[:width, width:]], axis=1)
    stacked = jnp.concatenate([coupling, left_data[width:] + right_data[:width]], axis=1)
    solved = jnp.linalg.solve(schur, stacked)
    interface = -solved[:, 2 * width:]
    outward = jnp.concatenate([left_map[:width, width:], right_map[width:, :width]], axis=0)
    parent_data = jnp.concatenate([left_data[:width], right_data[width:]], axis=0) + jnp.dot(outward, interface, precision=HIGHEST)
    parent_map = None
    if need_map:
        zeros = jnp.zeros((width, width), left_map.dtype)
        base = jnp.concatenate([jnp.concatenate([left_map[:width, :width], zeros], axis=1), jnp.concatenate([zeros, right_map[width:, width:]], axis=1)], axis=0)
        parent_map = base - jnp.dot(outward, solved[:, :2 * width], precision=HIGHEST)
    return (parent_map, parent_data, interface)

def level(maps, datas, need_map):
    count = maps.shape[0]
    paired_maps = maps.reshape((count // 2, 2) + maps.shape[1:])
    paired_data = datas.reshape((count // 2, 2) + datas.shape[1:])

    def one_pair(items):
        pair_maps, pair_data = items
        return jax.vmap(lambda lmap, ldat, rmap, rdat: merge(lmap, ldat, rmap, rdat, need_map))(pair_maps[0], pair_data[0], pair_maps[1], pair_data[1])
    return lax.map(one_pair, (paired_maps, paired_data))

def reference(velocity, field, conductivity, wall_flags, leaf_solution, leaf_dtn):
    slabs = leaf_solution.shape[1]
    depth = velocity.shape[4] // slabs

    def per_box(items):
        speed, magnet, conduct, flags, solution = items
        flow_x, flow_y, flow_z = currents(speed, magnet, conduct, flags)
        padded_z = jnp.pad(flow_z, ((0, 0), (0, 0), (1, 1), (0, 0)))
        source = divergence(flow_x, flow_y, padded_z).astype(jnp.bfloat16)
        sizex, sizey, total, snaps = source.shape
        blocks = source.reshape(sizex, sizey, slabs, depth, snaps).transpose(2, 0, 1, 3, 4).reshape(slabs, sizex * sizey * depth, snaps)
        return jnp.einsum('sfc,scr->sfr', solution.astype(jnp.float32), blocks.astype(jnp.float32))
    neumann_zero = lax.map(per_box, (velocity, field, conductivity, wall_flags, leaf_solution))
    map_one, neumann_one, interface_one = level(leaf_dtn, neumann_zero, True)
    unused, neumann_two, interface_two = level(map_one, neumann_one, False)
    return (jnp.repeat(interface_two, 4, axis=0), jnp.repeat(neumann_two, 4, axis=0))
```

```python
import functools

import jax
import jax.numpy as jnp
from jax import lax
from jax.experimental import pallas as pl
from jax.experimental.pallas import tpu as pltpu
from jax.sharding import PartitionSpec as P

WALL_RATIO = 8.0
SQUARINGS = 3
NEWTON_LIMIT = 12
CLOSE = 0.05
VMEM = pl.BlockSpec(memory_space=pltpu.VMEM)


def dot1(a, b):
    return jnp.dot(
        a.astype(jnp.bfloat16), b.astype(jnp.bfloat16), preferred_element_type=jnp.float32
    )


def halves(a):
    high = a.astype(jnp.bfloat16)
    return high, (a - high.astype(jnp.float32)).astype(jnp.bfloat16)


def dot3(a, b):
    ah, al = halves(a)
    bh, bl = halves(b)
    return dot1(ah, bh) + (dot1(ah, bl) + dot1(al, bh))


def eye(width):
    rows = lax.broadcasted_iota(jnp.int32, (width, width), 0)
    columns = lax.broadcasted_iota(jnp.int32, (width, width), 1)
    return (rows == columns).astype(jnp.float32)


def approximate_inverse(schur, inverse):
    width = schur.shape[0]
    unit = eye(width)
    matrix = schur[...]
    scale = jnp.sum(unit * matrix) / jnp.sum(matrix * matrix)
    power = unit - scale * matrix
    total = unit + power
    for _ in range(SQUARINGS):
        power = dot1(power, power)
        total = total + dot1(total, power)
    inverse[...] = scale * total

    def error():
        return unit - dot3(schur[...], inverse[...])

    first = error()

    def body(state):
        step, residual, norm = state
        inverse[...] += dot3(inverse[...], residual)
        residual = error()
        return step + 1, residual, jnp.sum(residual * residual)

    def far(state):
        step, residual, norm = state
        return jnp.logical_and(step < NEWTON_LIMIT, jnp.logical_not(norm < CLOSE * CLOSE))

    step, residual, norm = lax.while_loop(far, body, (0, first, jnp.sum(first * first)))
    good = norm < CLOSE * CLOSE

    @pl.when(good)
    def _():
        inverse[...] += dot1(inverse[...], residual)

    @pl.when(jnp.logical_not(good))
    def _():
        inverse[...] = schur[...]
        lane = lax.broadcasted_iota(jnp.int32, (width, width), 1)
        sublane = lax.broadcasted_iota(jnp.int32, (width, width), 0)

        def eliminate(k, carry):
            m = inverse[...]
            at = lane == k
            row = jnp.sum(jnp.where(sublane == k, m, 0.0), axis=0, keepdims=True)
            column = jnp.sum(jnp.where(at, m, 0.0), axis=1, keepdims=True)
            at_row = lax.broadcasted_iota(jnp.int32, (1, width), 1) == k
            pivot = jnp.sum(jnp.where(at_row, row, 0.0), axis=1, keepdims=True)
            scaled = jnp.where(at_row, 1.0, row) / pivot
            inverse[...] = jnp.where(sublane == k, scaled, jnp.where(at, 0.0, m) - column * scaled)
            return carry

        lax.fori_loop(0, width, eliminate, 0)


def solve(schur, inverse, b):
    y = dot1(inverse, b)
    return y + dot1(inverse, b - dot3(schur, y))


def roles():
    box = lax.axis_index("box")
    low, high = lax.rem(box, 2), lax.rem(lax.div(box, 2), 2)
    return low, low != high


def block(ref, row, column):
    width = ref.shape[0] // 2
    r = pl.multiple_of(row * width, width)
    c = pl.multiple_of(column * width, width)
    return ref[pl.ds(r, width), pl.ds(c, width)]


def face(ref, at):
    width = ref.shape[0] // 2
    return ref[pl.ds(pl.multiple_of(at * width, width), width), :]


def map_kernel(own, other, schur, inverse, parent, outward):
    low, inner = roles()
    mine, theirs = 1 - low, low
    schur[...] = block(own, mine, mine) + block(other, theirs, theirs)
    approximate_inverse(schur, inverse)
    inner_mi = jnp.where(inner, block(own, mine, low), block(other, theirs, mine))
    inner_im = jnp.where(inner, block(own, low, mine), block(other, mine, theirs))
    inner_ii = jnp.where(inner, block(own, low, low), block(other, mine, mine))
    outer_om = jnp.where(inner, block(other, mine, theirs), block(own, low, mine))
    weights = solve(schur[...], inverse[...], inner_mi)
    parent[...] = inner_ii - dot3(inner_im, weights)
    outward[...] = dot3(outer_om, weights)


def data_kernel(own, other, data, other_data, schur, inverse, inner_data, outer_data):
    low, inner = roles()
    mine, theirs = 1 - low, low
    b = face(data, mine) + face(other_data, theirs)
    interface = solve(schur[...], inverse[...], b)
    inner_im = jnp.where(inner, block(own, low, mine), block(other, mine, theirs))
    outer_om = jnp.where(inner, block(other, mine, theirs), block(own, low, mine))
    a, c = face(data, low), face(other_data, mine)
    inner_data[...] = jnp.where(inner, a, c) - dot3(inner_im, interface)
    outer_data[...] = jnp.where(inner, c, a) - dot3(outer_om, interface)


def second_map_kernel(parent, other_parent, schur, inverse):
    schur[...] = parent[...] + other_parent[...]
    approximate_inverse(schur, inverse)


def second_data_kernel(data, other_data, schur, inverse, outward, outer_data, interface, parent_data):
    y = solve(schur[...], inverse[...], data[...] + other_data[...])
    interface[...] = -y
    parent_data[...] = outer_data[...] + dot3(outward[...], y)


def local(kernel, outs, flops, *args):
    moved = sum(a.size * a.dtype.itemsize for a in args)
    return pl.pallas_call(
        kernel,
        out_shape=[jax.ShapeDtypeStruct(s, jnp.float32) for s in outs],
        in_specs=[VMEM] * len(args),
        out_specs=[VMEM] * len(outs),
        compiler_params=pltpu.CompilerParams(vmem_limit_bytes=32 * 1024 * 1024),
        cost_estimate=pl.CostEstimate(flops=flops, bytes_accessed=moved, transcendentals=0),
    )(*args)


def from_partner(block, axis, stride):
    count = lax.axis_size(axis)
    route = []
    for low in range(count):
        high = low | 1 << stride
        if high != low and high < count:
            route += [(low, high), (high, low)]
    return lax.ppermute(block, axis, route)


def padded_2(block, sides, width):
    for axis, dim in sides:
        count = lax.axis_size(axis)
        forward = [(i, i + 1) for i in range(count - 1)]
        backward = [(target, source) for source, target in forward]
        low = lax.ppermute(
            lax.slice_in_dim(block, block.shape[dim] - width, None, axis=dim), axis, forward
        )
        high = lax.ppermute(lax.slice_in_dim(block, 0, width, axis=dim), axis, backward)
        block = jnp.concatenate([low, block, high], axis=dim)
    return block


def currents(velocity, field, conductivity, wall_flags):
    sigma = conductivity * jnp.where(wall_flags == 1, WALL_RATIO, 1.0).astype(conductivity.dtype)
    speed = velocity.astype(jnp.float32)
    magnet = field[..., None]
    weight = sigma[..., None]
    elec_x = speed[1] * magnet[2] - speed[2] * magnet[1]
    elec_y = speed[2] * magnet[0] - speed[0] * magnet[2]
    elec_z = speed[0] * magnet[1] - speed[1] * magnet[0]
    return (weight * elec_x, weight * elec_y, weight * elec_z)


def divergence(flow_x, flow_y, padded_z):
    padded_x = jnp.pad(flow_x, ((1, 1), (0, 0), (0, 0), (0, 0)))
    padded_y = jnp.pad(flow_y, ((0, 0), (1, 1), (0, 0), (0, 0)))
    return 0.5 * (
        padded_x[2:]
        - padded_x[:-2]
        + (padded_y[:, 2:] - padded_y[:, :-2])
        + (padded_z[:, :, 2:] - padded_z[:, :, :-2])
    )


def on_device(velocity, field, conductivity, wall_flags, leaf_solution, leaf_dtn):
    dtn_map = leaf_dtn[0, 0]
    width = dtn_map.shape[0] // 2
    square = (width, width)
    other_map = from_partner(dtn_map, "box", 0)
    flow_x, flow_y, flow_z = currents(velocity[0], field[0], conductivity[0], wall_flags[0])
    solution_map = leaf_solution[0, 0]
    sizex, sizey, depth, snaps = flow_x.shape
    thin = (width, snaps)
    cell_count = sizex * sizey * depth
    padded = padded_2(flow_z, (("slab", 2),), 1)
    source = divergence(flow_x, flow_y, padded).astype(jnp.bfloat16)
    neumann = jnp.dot(
        solution_map, source.reshape(cell_count, snaps), preferred_element_type=jnp.float32
    )
    other_neumann = from_partner(neumann, "box", 0)

    cube = 2 * width**3
    schur, inverse, parent, outward = local(
        map_kernel, [square] * 4, 30 * cube, dtn_map, other_map
    )
    other_parent = from_partner(parent, "box", 1)
    schur_two, inverse_two = local(
        second_map_kernel, [square] * 2, 20 * cube, parent, other_parent
    )
    inner_data, outer_data = local(
        data_kernel, [thin] * 2, 6 * cube, dtn_map, other_map, neumann, other_neumann, schur, inverse
    )
    other_inner = from_partner(inner_data, "box", 1)
    interface, own_side = local(
        second_data_kernel,
        [thin] * 2,
        4 * cube,
        inner_data,
        other_inner,
        schur_two,
        inverse_two,
        outward,
        outer_data,
    )
    other_side = from_partner(own_side, "box", 1)
    left = lax.axis_index("box") >> 1 & 1 == 0
    first = jnp.where(left, own_side, other_side)
    second = jnp.where(left, other_side, own_side)
    return (interface[None, None], jnp.concatenate([first, second], axis=0)[None, None])


def solution(mesh):
    return jax.shard_map(
        on_device,
        mesh=mesh,
        in_specs=(
            P("box", None, None, None, "slab", None),
            P("box", None, None, None, "slab"),
            P("box", None, None, "slab"),
            P("box", None, None, "slab"),
            P("box", "slab", None, None),
            P("box", "slab", None, None),
        ),
        out_specs=(P("box", "slab", None, None), P("box", "slab", None, None)),
        check_vma=False,
    )
```

```python
import functools

import jax
import jax.numpy as jnp
from jax import lax
from jax.experimental import pallas as pl
from jax.experimental.pallas import tpu as pltpu
from jax.sharding import PartitionSpec as P

WALL_RATIO = 8.0
SQUARINGS = 3
NEWTON_LIMIT = 12
CLOSE = 0.05
MESH = pl.DeviceIdType.MESH
VMEM = pl.BlockSpec(memory_space=pltpu.VMEM)


def dot1(a, b):
    return jnp.dot(
        a.astype(jnp.bfloat16), b.astype(jnp.bfloat16), preferred_element_type=jnp.float32
    )


def halves(a):
    high = a.astype(jnp.bfloat16)
    return high, (a - high.astype(jnp.float32)).astype(jnp.bfloat16)


def dot3(a, b):
    ah, al = halves(a)
    bh, bl = halves(b)
    return dot1(ah, bh) + (dot1(ah, bl) + dot1(al, bh))


def eye(width):
    rows = lax.broadcasted_iota(jnp.int32, (width, width), 0)
    columns = lax.broadcasted_iota(jnp.int32, (width, width), 1)
    return (rows == columns).astype(jnp.float32)


def approximate_inverse(schur, inverse):
    width = schur.shape[0]
    unit = eye(width)
    matrix = schur[...]
    scale = jnp.sum(unit * matrix) / jnp.sum(matrix * matrix)
    power = unit - scale * matrix
    total = unit + power
    for _ in range(SQUARINGS):
        power = dot1(power, power)
        total = total + dot1(total, power)
    inverse[...] = scale * total

    def error():
        return unit - dot3(schur[...], inverse[...])

    first = error()

    def body(state):
        step, residual, norm = state
        inverse[...] += dot3(inverse[...], residual)
        residual = error()
        return step + 1, residual, jnp.sum(residual * residual)

    def far(state):
        step, residual, norm = state
        return jnp.logical_and(step < NEWTON_LIMIT, jnp.logical_not(norm < CLOSE * CLOSE))

    step, residual, norm = lax.while_loop(far, body, (0, first, jnp.sum(first * first)))
    good = norm < CLOSE * CLOSE

    @pl.when(good)
    def _():
        inverse[...] += dot1(inverse[...], residual)

    @pl.when(jnp.logical_not(good))
    def _():
        inverse[...] = schur[...]
        lane = lax.broadcasted_iota(jnp.int32, (width, width), 1)
        sublane = lax.broadcasted_iota(jnp.int32, (width, width), 0)

        def eliminate(k, carry):
            m = inverse[...]
            at = lane == k
            row = jnp.sum(jnp.where(sublane == k, m, 0.0), axis=0, keepdims=True)
            column = jnp.sum(jnp.where(at, m, 0.0), axis=1, keepdims=True)
            at_row = lax.broadcasted_iota(jnp.int32, (1, width), 1) == k
            pivot = jnp.sum(jnp.where(at_row, row, 0.0), axis=1, keepdims=True)
            scaled = jnp.where(at_row, 1.0, row) / pivot
            inverse[...] = jnp.where(sublane == k, scaled, jnp.where(at, 0.0, m) - column * scaled)
            return carry

        lax.fori_loop(0, width, eliminate, 0)


def solve(schur, inverse, b):
    y = dot1(inverse, b)
    return y + dot1(inverse, b - dot3(schur, y))


def roles():
    box = lax.axis_index("box")
    low, high = lax.rem(box, 2), lax.rem(lax.div(box, 2), 2)
    return low, low != high


def block(ref, row, column):
    width = ref.shape[0] // 2
    r = pl.multiple_of(row * width, width)
    c = pl.multiple_of(column * width, width)
    return ref[pl.ds(r, width), pl.ds(c, width)]


def face(ref, at):
    width = ref.shape[0] // 2
    return ref[pl.ds(pl.multiple_of(at * width, width), width), :]


def map_kernel(own, other, schur, inverse, parent, outward):
    low, inner = roles()
    mine, theirs = 1 - low, low
    schur[...] = block(own, mine, mine) + block(other, theirs, theirs)
    approximate_inverse(schur, inverse)
    inner_mi = jnp.where(inner, block(own, mine, low), block(other, theirs, mine))
    inner_im = jnp.where(inner, block(own, low, mine), block(other, mine, theirs))
    inner_ii = jnp.where(inner, block(own, low, low), block(other, mine, mine))
    outer_om = jnp.where(inner, block(other, mine, theirs), block(own, low, mine))
    weights = solve(schur[...], inverse[...], inner_mi)
    parent[...] = inner_ii - dot3(inner_im, weights)
    outward[...] = dot3(outer_om, weights)


def data_kernel(own, other, data, other_data, schur, inverse, inner_data, outer_data):
    low, inner = roles()
    mine, theirs = 1 - low, low
    b = face(data, mine) + face(other_data, theirs)
    interface = solve(schur[...], inverse[...], b)
    inner_im = jnp.where(inner, block(own, low, mine), block(other, mine, theirs))
    outer_om = jnp.where(inner, block(other, mine, theirs), block(own, low, mine))
    a, c = face(data, low), face(other_data, mine)
    inner_data[...] = jnp.where(inner, a, c) - dot3(inner_im, interface)
    outer_data[...] = jnp.where(inner, c, a) - dot3(outer_om, interface)


def second_map_kernel(parent, other_parent, schur, inverse):
    schur[...] = parent[...] + other_parent[...]
    approximate_inverse(schur, inverse)


def second_data_kernel(data, other_data, schur, inverse, outward, outer_data, interface, parent_data):
    y = solve(schur[...], inverse[...], data[...] + other_data[...])
    interface[...] = -y
    parent_data[...] = outer_data[...] + dot3(outward[...], y)


def local(kernel, outs, flops, *args):
    moved = sum(a.size * a.dtype.itemsize for a in args)
    return pl.pallas_call(
        kernel,
        out_shape=[jax.ShapeDtypeStruct(s, jnp.float32) for s in outs],
        in_specs=[VMEM] * len(args),
        out_specs=[VMEM] * len(outs),
        compiler_params=pltpu.CompilerParams(vmem_limit_bytes=32 * 1024 * 1024),
        cost_estimate=pl.CostEstimate(flops=flops, bytes_accessed=moved, transcendentals=0),
    )(*args)


def from_partner(block, axis, stride):
    count = lax.axis_size(axis)
    route = []
    for low in range(count):
        high = low | 1 << stride
        if high != low and high < count:
            route += [(low, high), (high, low)]
    return lax.ppermute(block, axis, route)


def front_kernel(velocity, field, conductivity, wall_flags, solution_map, neumann, flow_x, part, ends, low_halo, high_halo, source, send_sem, receive_sem):
    slab = lax.axis_index("slab")
    count = lax.axis_size("slab")
    has_low, has_high = slab > 0, slab < count - 1
    lower = lax.max(slab - 1, 0)
    upper = lax.min(slab + 1, count - 1)
    barrier = pltpu.get_barrier_semaphore()

    @pl.when(has_low)
    def _():
        pl.semaphore_signal(barrier, inc=1, device_id={"slab": lower}, device_id_type=MESH)

    @pl.when(has_high)
    def _():
        pl.semaphore_signal(barrier, inc=1, device_id={"slab": upper}, device_id_type=MESH)

    sizex, sizey, depth, snaps = part.shape
    plane = (sizey, depth, snaps)
    at_z = lax.broadcasted_iota(jnp.int32, plane, 1)
    first, last = at_z == 0, at_z == depth - 1
    none = jnp.zeros((1, depth, snaps), jnp.float32)
    flow_x[0] = jnp.zeros(plane, jnp.float32)
    flow_x[sizex + 1] = jnp.zeros(plane, jnp.float32)

    def moved(a, steps):
        flat = pltpu.roll(a.reshape(sizey * depth, snaps), steps, 0)
        return flat.reshape(plane)

    def current(x, carry):
        sigma = conductivity[x] * jnp.where(wall_flags[x] == 1, WALL_RATIO, 1.0)
        m0, m1, m2 = [
            jnp.broadcast_to((sigma * field[d, x])[:, :, None], plane) for d in range(3)
        ]
        v0, v1, v2 = [velocity[d, x].astype(jnp.float32) for d in range(3)]
        flow_x[x + 1] = v1 * m2 - v2 * m1
        flow_y = v2 * m0 - v0 * m2
        flow_z = v0 * m1 - v1 * m0
        ends[0, x] = jnp.sum(jnp.where(first, flow_z, 0.0), axis=1, keepdims=True)
        ends[1, x] = jnp.sum(jnp.where(last, flow_z, 0.0), axis=1, keepdims=True)
        after = jnp.where(last, 0.0, moved(flow_z, sizey * depth - 1))
        before = jnp.where(first, 0.0, moved(flow_z, 1))
        across = jnp.concatenate([flow_y[1:], none]) - jnp.concatenate([none, flow_y[:-1]])
        part[x] = across + (after - before)
        return carry

    lax.fori_loop(0, sizex, current, 0)
    pl.semaphore_wait(barrier, has_low.astype(jnp.int32) + has_high.astype(jnp.int32))
    down = pltpu.make_async_remote_copy(
        src_ref=ends.at[0],
        dst_ref=high_halo,
        send_sem=send_sem.at[0],
        recv_sem=receive_sem.at[0],
        device_id={"slab": lower},
        device_id_type=MESH,
    )
    up = pltpu.make_async_remote_copy(
        src_ref=ends.at[1],
        dst_ref=low_halo,
        send_sem=send_sem.at[1],
        recv_sem=receive_sem.at[1],
        device_id={"slab": upper},
        device_id_type=MESH,
    )

    @pl.when(has_low)
    def _():
        down.start()

    @pl.when(jnp.logical_not(has_low))
    def _():
        low_halo[...] = jnp.zeros_like(low_halo)

    @pl.when(has_high)
    def _():
        up.start()

    @pl.when(jnp.logical_not(has_high))
    def _():
        high_halo[...] = jnp.zeros_like(high_halo)

    def along(x, carry):
        part[x] += flow_x[x + 2] - flow_x[x]
        return carry

    lax.fori_loop(0, sizex, along, 0)

    @pl.when(has_low)
    def _():
        up.wait_recv()
        down.wait_send()

    @pl.when(has_high)
    def _():
        down.wait_recv()
        up.wait_send()

    def finish(x, carry):
        low = jnp.broadcast_to(low_halo[x], plane)
        high = jnp.broadcast_to(high_halo[x], plane)
        ending = jnp.where(last, high, 0.0) - jnp.where(first, low, 0.0)
        rows = sizey * depth
        whole = (0.5 * (part[x] + ending)).reshape(rows, snaps)
        source[pl.ds(pl.multiple_of(x * rows, rows), rows), :] = whole.astype(jnp.bfloat16)
        return carry

    lax.fori_loop(0, sizex, finish, 0)
    neumann[...] = jnp.dot(solution_map[...], source[...], preferred_element_type=jnp.float32)


def front(velocity, field, conductivity, wall_flags, solution_map):
    _, sizex, sizey, depth, snaps = velocity.shape
    f32 = jnp.float32
    return pl.pallas_call(
        front_kernel,
        out_shape=jax.ShapeDtypeStruct((solution_map.shape[0], snaps), f32),
        in_specs=[VMEM] * 5,
        out_specs=VMEM,
        scratch_shapes=[
            pltpu.VMEM((sizex + 2, sizey, depth, snaps), f32),
            pltpu.VMEM((sizex, sizey, depth, snaps), f32),
            pltpu.VMEM((2, sizex, sizey, 1, snaps), f32),
            pltpu.VMEM((sizex, sizey, 1, snaps), f32),
            pltpu.VMEM((sizex, sizey, 1, snaps), f32),
            pltpu.VMEM((sizex * sizey * depth, snaps), jnp.bfloat16),
            pltpu.SemaphoreType.DMA((2,)),
            pltpu.SemaphoreType.DMA((2,)),
        ],
        compiler_params=pltpu.CompilerParams(
            collective_id=0, has_side_effects=True, vmem_limit_bytes=40 * 1024 * 1024
        ),
        cost_estimate=pl.CostEstimate(
            flops=2 * solution_map.size * snaps, bytes_accessed=4 * 2**20, transcendentals=0
        ),
    )(velocity, field, conductivity, wall_flags, solution_map)


def on_device(velocity, field, conductivity, wall_flags, leaf_solution, leaf_dtn):
    dtn_map = leaf_dtn[0, 0]
    width = dtn_map.shape[0] // 2
    square = (width, width)
    other_map = from_partner(dtn_map, "box", 0)
    neumann = front(velocity[0], field[0], conductivity[0], wall_flags[0], leaf_solution[0, 0])
    thin = (width, neumann.shape[1])
    other_neumann = from_partner(neumann, "box", 0)

    cube = 2 * width**3
    schur, inverse, parent, outward = local(
        map_kernel, [square] * 4, 30 * cube, dtn_map, other_map
    )
    other_parent = from_partner(parent, "box", 1)
    schur_two, inverse_two = local(
        second_map_kernel, [square] * 2, 20 * cube, parent, other_parent
    )
    inner_data, outer_data = local(
        data_kernel, [thin] * 2, 6 * cube, dtn_map, other_map, neumann, other_neumann, schur, inverse
    )
    other_inner = from_partner(inner_data, "box", 1)
    interface, own_side = local(
        second_data_kernel,
        [thin] * 2,
        4 * cube,
        inner_data,
        other_inner,
        schur_two,
        inverse_two,
        outward,
        outer_data,
    )
    other_side = from_partner(own_side, "box", 1)
    left = lax.axis_index("box") >> 1 & 1 == 0
    first = jnp.where(left, own_side, other_side)
    second = jnp.where(left, other_side, own_side)
    return (interface[None, None], jnp.concatenate([first, second], axis=0)[None, None])


def solution(mesh):
    return jax.shard_map(
        on_device,
        mesh=mesh,
        in_specs=(
            P("box", None, None, None, "slab", None),
            P("box", None, None, None, "slab"),
            P("box", None, None, "slab"),
            P("box", None, None, "slab"),
            P("box", "slab", None, None),
            P("box", "slab", None, None),
        ),
        out_specs=(P("box", "slab", None, None), P("box", "slab", None, None)),
        check_vma=False,
    )
```

```python
import functools

import jax
import jax.numpy as jnp
from jax import lax
from jax.experimental import pallas as pl
from jax.experimental.pallas import tpu as pltpu
from jax.sharding import PartitionSpec as P

WALL_RATIO = 8.0
SQUARINGS = 3
NEWTON_LIMIT = 12
CLOSE = 0.05
MESH = pl.DeviceIdType.MESH
VMEM = pl.BlockSpec(memory_space=pltpu.VMEM)


def dot1(a, b):
    return jnp.dot(
        a.astype(jnp.bfloat16), b.astype(jnp.bfloat16), preferred_element_type=jnp.float32
    )


def halves(a):
    high = a.astype(jnp.bfloat16)
    return high, (a - high.astype(jnp.float32)).astype(jnp.bfloat16)


def dot3(a, b):
    ah, al = halves(a)
    bh, bl = halves(b)
    return dot1(ah, bh) + (dot1(ah, bl) + dot1(al, bh))


def eye(width):
    rows = lax.broadcasted_iota(jnp.int32, (width, width), 0)
    columns = lax.broadcasted_iota(jnp.int32, (width, width), 1)
    return (rows == columns).astype(jnp.float32)


def approximate_inverse(schur, inverse):
    width = schur.shape[0]
    unit = eye(width)
    matrix = schur[...]
    scale = jnp.sum(unit * matrix) / jnp.sum(matrix * matrix)
    power = unit - scale * matrix
    total = unit + power
    for _ in range(SQUARINGS):
        power = dot1(power, power)
        total = total + dot1(total, power)
    inverse[...] = scale * total

    def error():
        return unit - dot3(schur[...], inverse[...])

    first = error()

    def body(state):
        step, residual, norm = state
        inverse[...] += dot3(inverse[...], residual)
        residual = error()
        return step + 1, residual, jnp.sum(residual * residual)

    def far(state):
        step, residual, norm = state
        return jnp.logical_and(step < NEWTON_LIMIT, jnp.logical_not(norm < CLOSE * CLOSE))

    step, residual, norm = lax.while_loop(far, body, (0, first, jnp.sum(first * first)))
    good = norm < CLOSE * CLOSE

    @pl.when(good)
    def _():
        inverse[...] += dot1(inverse[...], residual)

    @pl.when(jnp.logical_not(good))
    def _():
        inverse[...] = schur[...]
        lane = lax.broadcasted_iota(jnp.int32, (width, width), 1)
        sublane = lax.broadcasted_iota(jnp.int32, (width, width), 0)

        def eliminate(k, carry):
            m = inverse[...]
            at = lane == k
            row = jnp.sum(jnp.where(sublane == k, m, 0.0), axis=0, keepdims=True)
            column = jnp.sum(jnp.where(at, m, 0.0), axis=1, keepdims=True)
            at_row = lax.broadcasted_iota(jnp.int32, (1, width), 1) == k
            pivot = jnp.sum(jnp.where(at_row, row, 0.0), axis=1, keepdims=True)
            scaled = jnp.where(at_row, 1.0, row) / pivot
            inverse[...] = jnp.where(sublane == k, scaled, jnp.where(at, 0.0, m) - column * scaled)
            return carry

        lax.fori_loop(0, width, eliminate, 0)


def solve(schur, inverse, b):
    y = dot1(inverse, b)
    return y + dot1(inverse, b - dot3(schur, y))


def roles():
    box = lax.axis_index("box")
    low, high = lax.rem(box, 2), lax.rem(lax.div(box, 2), 2)
    return low, low != high


def block(ref, row, column):
    width = ref.shape[0] // 2
    r = pl.multiple_of(row * width, width)
    c = pl.multiple_of(column * width, width)
    return ref[pl.ds(r, width), pl.ds(c, width)]


def face(ref, at):
    width = ref.shape[0] // 2
    return ref[pl.ds(pl.multiple_of(at * width, width), width), :]


def map_kernel(own, other, schur, inverse, parent, outward):
    low, inner = roles()
    mine, theirs = 1 - low, low
    schur[...] = block(own, mine, mine) + block(other, theirs, theirs)
    approximate_inverse(schur, inverse)
    inner_mi = jnp.where(inner, block(own, mine, low), block(other, theirs, mine))
    inner_im = jnp.where(inner, block(own, low, mine), block(other, mine, theirs))
    inner_ii = jnp.where(inner, block(own, low, low), block(other, mine, mine))
    outer_om = jnp.where(inner, block(other, mine, theirs), block(own, low, mine))
    weights = solve(schur[...], inverse[...], inner_mi)
    parent[...] = inner_ii - dot3(inner_im, weights)
    outward[...] = dot3(outer_om, weights)


def data_kernel(own, other, data, other_data, schur, inverse, inner_data, outer_data):
    low, inner = roles()
    mine, theirs = 1 - low, low
    b = face(data, mine) + face(other_data, theirs)
    interface = solve(schur[...], inverse[...], b)
    inner_im = jnp.where(inner, block(own, low, mine), block(other, mine, theirs))
    outer_om = jnp.where(inner, block(other, mine, theirs), block(own, low, mine))
    a, c = face(data, low), face(other_data, mine)
    inner_data[...] = jnp.where(inner, a, c) - dot3(inner_im, interface)
    outer_data[...] = jnp.where(inner, c, a) - dot3(outer_om, interface)


def second_map_kernel(parent, other_parent, schur, inverse):
    schur[...] = parent[...] + other_parent[...]
    approximate_inverse(schur, inverse)


def second_data_kernel(data, other_data, schur, inverse, outward, outer_data, interface, parent_data):
    y = solve(schur[...], inverse[...], data[...] + other_data[...])
    interface[...] = -y
    parent_data[...] = outer_data[...] + dot3(outward[...], y)


def local(kernel, outs, flops, *args):
    moved = sum(a.size * a.dtype.itemsize for a in args)
    return pl.pallas_call(
        kernel,
        out_shape=[jax.ShapeDtypeStruct(s, jnp.float32) for s in outs],
        in_specs=[VMEM] * len(args),
        out_specs=[VMEM] * len(outs),
        compiler_params=pltpu.CompilerParams(vmem_limit_bytes=32 * 1024 * 1024),
        cost_estimate=pl.CostEstimate(flops=flops, bytes_accessed=moved, transcendentals=0),
    )(*args)


def from_partner(block, axis, stride):
    count = lax.axis_size(axis)
    route = []
    for low in range(count):
        high = low | 1 << stride
        if high != low and high < count:
            route += [(low, high), (high, low)]
    return lax.ppermute(block, axis, route)


def front_kernel(*refs):
    far, (neumann,), near = refs[:5], refs[5:6], refs[6:11]
    flow_x, part, ends, low_halo, high_halo, source, send_sem, receive_sem, load_sem = refs[11:]
    velocity, field, conductivity, wall_flags, solution_map = near
    loads = [pltpu.make_async_copy(far[i], near[i], load_sem.at[i]) for i in range(5)]
    for i in (1, 2, 3, 0, 4):
        loads[i].start()
    slab = lax.axis_index("slab")
    count = lax.axis_size("slab")
    has_low, has_high = slab > 0, slab < count - 1
    lower = lax.max(slab - 1, 0)
    upper = lax.min(slab + 1, count - 1)
    barrier = pltpu.get_barrier_semaphore()

    @pl.when(has_low)
    def _():
        pl.semaphore_signal(barrier, inc=1, device_id={"slab": lower}, device_id_type=MESH)

    @pl.when(has_high)
    def _():
        pl.semaphore_signal(barrier, inc=1, device_id={"slab": upper}, device_id_type=MESH)

    sizex, sizey, depth, snaps = part.shape
    plane = (sizey, depth, snaps)
    at_z = lax.broadcasted_iota(jnp.int32, plane, 1)
    first, last = at_z == 0, at_z == depth - 1
    none = jnp.zeros((1, depth, snaps), jnp.float32)
    flow_x[0] = jnp.zeros(plane, jnp.float32)
    flow_x[sizex + 1] = jnp.zeros(plane, jnp.float32)

    def moved(a, steps):
        flat = pltpu.roll(a.reshape(sizey * depth, snaps), steps, 0)
        return flat.reshape(plane)

    def current(x, carry):
        sigma = conductivity[x] * jnp.where(wall_flags[x] == 1, WALL_RATIO, 1.0)
        m0, m1, m2 = [
            jnp.broadcast_to((sigma * field[d, x])[:, :, None], plane) for d in range(3)
        ]
        v0, v1, v2 = [velocity[d, x].astype(jnp.float32) for d in range(3)]
        flow_x[x + 1] = v1 * m2 - v2 * m1
        flow_y = v2 * m0 - v0 * m2
        flow_z = v0 * m1 - v1 * m0
        ends[0, x] = jnp.sum(jnp.where(first, flow_z, 0.0), axis=1, keepdims=True)
        ends[1, x] = jnp.sum(jnp.where(last, flow_z, 0.0), axis=1, keepdims=True)
        after = jnp.where(last, 0.0, moved(flow_z, sizey * depth - 1))
        before = jnp.where(first, 0.0, moved(flow_z, 1))
        across = jnp.concatenate([flow_y[1:], none]) - jnp.concatenate([none, flow_y[:-1]])
        part[x] = across + (after - before)
        return carry

    for i in range(4):
        loads[i].wait()
    lax.fori_loop(0, sizex, current, 0)
    pl.semaphore_wait(barrier, has_low.astype(jnp.int32) + has_high.astype(jnp.int32))
    down = pltpu.make_async_remote_copy(
        src_ref=ends.at[0],
        dst_ref=high_halo,
        send_sem=send_sem.at[0],
        recv_sem=receive_sem.at[0],
        device_id={"slab": lower},
        device_id_type=MESH,
    )
    up = pltpu.make_async_remote_copy(
        src_ref=ends.at[1],
        dst_ref=low_halo,
        send_sem=send_sem.at[1],
        recv_sem=receive_sem.at[1],
        device_id={"slab": upper},
        device_id_type=MESH,
    )

    @pl.when(has_low)
    def _():
        down.start()

    @pl.when(jnp.logical_not(has_low))
    def _():
        low_halo[...] = jnp.zeros_like(low_halo)

    @pl.when(has_high)
    def _():
        up.start()

    @pl.when(jnp.logical_not(has_high))
    def _():
        high_halo[...] = jnp.zeros_like(high_halo)

    def along(x, carry):
        part[x] += flow_x[x + 2] - flow_x[x]
        return carry

    lax.fori_loop(0, sizex, along, 0)

    @pl.when(has_low)
    def _():
        up.wait_recv()
        down.wait_send()

    @pl.when(has_high)
    def _():
        down.wait_recv()
        up.wait_send()

    def finish(x, carry):
        low = jnp.broadcast_to(low_halo[x], plane)
        high = jnp.broadcast_to(high_halo[x], plane)
        ending = jnp.where(last, high, 0.0) - jnp.where(first, low, 0.0)
        rows = sizey * depth
        whole = (0.5 * (part[x] + ending)).reshape(rows, snaps)
        source[pl.ds(pl.multiple_of(x * rows, rows), rows), :] = whole.astype(jnp.bfloat16)
        return carry

    lax.fori_loop(0, sizex, finish, 0)
    loads[4].wait()
    neumann[...] = jnp.dot(solution_map[...], source[...], preferred_element_type=jnp.float32)


def front(velocity, field, conductivity, wall_flags, solution_map):
    arrays = (velocity, field, conductivity, wall_flags, solution_map)
    _, sizex, sizey, depth, snaps = velocity.shape
    f32 = jnp.float32
    return pl.pallas_call(
        front_kernel,
        out_shape=jax.ShapeDtypeStruct((solution_map.shape[0], snaps), f32),
        in_specs=[pl.BlockSpec(memory_space=pltpu.MemorySpace.HBM)] * 5,
        out_specs=VMEM,
        scratch_shapes=[pltpu.VMEM(a.shape, a.dtype) for a in arrays]
        + [
            pltpu.VMEM((sizex + 2, sizey, depth, snaps), f32),
            pltpu.VMEM((sizex, sizey, depth, snaps), f32),
            pltpu.VMEM((2, sizex, sizey, 1, snaps), f32),
            pltpu.VMEM((sizex, sizey, 1, snaps), f32),
            pltpu.VMEM((sizex, sizey, 1, snaps), f32),
            pltpu.VMEM((sizex * sizey * depth, snaps), jnp.bfloat16),
            pltpu.SemaphoreType.DMA((2,)),
            pltpu.SemaphoreType.DMA((2,)),
            pltpu.SemaphoreType.DMA((5,)),
        ],
        compiler_params=pltpu.CompilerParams(
            collective_id=0, has_side_effects=True, vmem_limit_bytes=40 * 1024 * 1024
        ),
        cost_estimate=pl.CostEstimate(
            flops=2 * solution_map.size * snaps, bytes_accessed=4 * 2**20, transcendentals=0
        ),
    )(*arrays)


def on_device(velocity, field, conductivity, wall_flags, leaf_solution, leaf_dtn):
    dtn_map = leaf_dtn[0, 0]
    width = dtn_map.shape[0] // 2
    square = (width, width)
    other_map = from_partner(dtn_map, "box", 0)
    cube = 2 * width**3
    schur, inverse, parent, outward = local(
        map_kernel, [square] * 4, 30 * cube, dtn_map, other_map
    )
    velocity, parent = lax.optimization_barrier((velocity, parent))
    neumann = front(velocity[0], field[0], conductivity[0], wall_flags[0], leaf_solution[0, 0])
    thin = (width, neumann.shape[1])
    other_neumann = from_partner(neumann, "box", 0)
    other_parent = from_partner(parent, "box", 1)
    schur_two, inverse_two = local(
        second_map_kernel, [square] * 2, 20 * cube, parent, other_parent
    )
    inner_data, outer_data = local(
        data_kernel, [thin] * 2, 6 * cube, dtn_map, other_map, neumann, other_neumann, schur, inverse
    )
    other_inner = from_partner(inner_data, "box", 1)
    interface, own_side = local(
        second_data_kernel,
        [thin] * 2,
        4 * cube,
        inner_data,
        other_inner,
        schur_two,
        inverse_two,
        outward,
        outer_data,
    )
    other_side = from_partner(own_side, "box", 1)
    left = lax.axis_index("box") >> 1 & 1 == 0
    first = jnp.where(left, own_side, other_side)
    second = jnp.where(left, other_side, own_side)
    return (interface[None, None], jnp.concatenate([first, second], axis=0)[None, None])


def solution(mesh):
    return jax.shard_map(
        on_device,
        mesh=mesh,
        in_specs=(
            P("box", None, None, None, "slab", None),
            P("box", None, None, None, "slab"),
            P("box", None, None, "slab"),
            P("box", None, None, "slab"),
            P("box", "slab", None, None),
            P("box", "slab", None, None),
        ),
        out_specs=(P("box", "slab", None, None), P("box", "slab", None, None)),
        check_vma=False,
    )
```

```python
import functools

import jax
import jax.numpy as jnp
from jax import lax
from jax.experimental import pallas as pl
from jax.experimental.pallas import tpu as pltpu
from jax.sharding import PartitionSpec as P

WALL_RATIO = 8.0
SQUARINGS = 3
NEWTON_LIMIT = 12
CLOSE = 0.05
MESH = pl.DeviceIdType.MESH
VMEM = pl.BlockSpec(memory_space=pltpu.VMEM)


def dot1(a, b):
    return jnp.dot(
        a.astype(jnp.bfloat16), b.astype(jnp.bfloat16), preferred_element_type=jnp.float32
    )


def halves(a):
    high = a.astype(jnp.bfloat16)
    return high, (a - high.astype(jnp.float32)).astype(jnp.bfloat16)


def dot3(a, b):
    ah, al = halves(a)
    bh, bl = halves(b)
    return dot1(ah, bh) + (dot1(ah, bl) + dot1(al, bh))


def eye(width):
    rows = lax.broadcasted_iota(jnp.int32, (width, width), 0)
    columns = lax.broadcasted_iota(jnp.int32, (width, width), 1)
    return (rows == columns).astype(jnp.float32)


def approximate_inverse(schur, inverse):
    width = schur.shape[0]
    unit = eye(width)
    matrix = schur[...]
    scale = jnp.sum(unit * matrix) / jnp.sum(matrix * matrix)
    power = unit - scale * matrix
    total = unit + power
    for _ in range(SQUARINGS):
        power = dot1(power, power)
        total = total + dot1(total, power)
    inverse[...] = scale * total

    def error():
        return unit - dot3(schur[...], inverse[...])

    first = error()

    def body(state):
        step, residual, norm = state
        inverse[...] += dot3(inverse[...], residual)
        residual = error()
        return step + 1, residual, jnp.sum(residual * residual)

    def far(state):
        step, residual, norm = state
        return jnp.logical_and(step < NEWTON_LIMIT, jnp.logical_not(norm < CLOSE * CLOSE))

    step, residual, norm = lax.while_loop(far, body, (0, first, jnp.sum(first * first)))
    good = norm < CLOSE * CLOSE

    @pl.when(good)
    def _():
        inverse[...] += dot1(inverse[...], residual)

    @pl.when(jnp.logical_not(good))
    def _():
        inverse[...] = schur[...]
        lane = lax.broadcasted_iota(jnp.int32, (width, width), 1)
        sublane = lax.broadcasted_iota(jnp.int32, (width, width), 0)

        def eliminate(k, carry):
            m = inverse[...]
            at = lane == k
            row = jnp.sum(jnp.where(sublane == k, m, 0.0), axis=0, keepdims=True)
            column = jnp.sum(jnp.where(at, m, 0.0), axis=1, keepdims=True)
            at_row = lax.broadcasted_iota(jnp.int32, (1, width), 1) == k
            pivot = jnp.sum(jnp.where(at_row, row, 0.0), axis=1, keepdims=True)
            scaled = jnp.where(at_row, 1.0, row) / pivot
            inverse[...] = jnp.where(sublane == k, scaled, jnp.where(at, 0.0, m) - column * scaled)
            return carry

        lax.fori_loop(0, width, eliminate, 0)


def solve(schur, inverse, b):
    y = dot1(inverse, b)
    return y + dot1(inverse, b - dot3(schur, y))


def roles():
    box = lax.axis_index("box")
    low, high = lax.rem(box, 2), lax.rem(lax.div(box, 2), 2)
    return low, low != high


def block(ref, row, column):
    width = ref.shape[0] // 2
    r = pl.multiple_of(row * width, width)
    c = pl.multiple_of(column * width, width)
    return ref[pl.ds(r, width), pl.ds(c, width)]


def face(ref, at):
    width = ref.shape[0] // 2
    return ref[pl.ds(pl.multiple_of(at * width, width), width), :]


def map_kernel(own, other, schur, inverse, parent, outward):
    low, inner = roles()
    mine, theirs = 1 - low, low
    schur[...] = block(own, mine, mine) + block(other, theirs, theirs)
    approximate_inverse(schur, inverse)
    inner_mi = jnp.where(inner, block(own, mine, low), block(other, theirs, mine))
    inner_im = jnp.where(inner, block(own, low, mine), block(other, mine, theirs))
    inner_ii = jnp.where(inner, block(own, low, low), block(other, mine, mine))
    outer_om = jnp.where(inner, block(other, mine, theirs), block(own, low, mine))
    weights = solve(schur[...], inverse[...], inner_mi)
    parent[...] = inner_ii - dot3(inner_im, weights)
    outward[...] = dot3(outer_om, weights)


def data_kernel(own, other, data, other_data, schur, inverse, inner_data, outer_data):
    low, inner = roles()
    mine, theirs = 1 - low, low
    b = face(data, mine) + face(other_data, theirs)
    interface = solve(schur[...], inverse[...], b)
    inner_im = jnp.where(inner, block(own, low, mine), block(other, mine, theirs))
    outer_om = jnp.where(inner, block(other, mine, theirs), block(own, low, mine))
    a, c = face(data, low), face(other_data, mine)
    inner_data[...] = jnp.where(inner, a, c) - dot3(inner_im, interface)
    outer_data[...] = jnp.where(inner, c, a) - dot3(outer_om, interface)


def second_map_kernel(parent, other_parent, schur, inverse):
    schur[...] = parent[...] + other_parent[...]
    approximate_inverse(schur, inverse)


def second_data_kernel(data, other_data, schur, inverse, outward, outer_data, interface, parent_data):
    y = solve(schur[...], inverse[...], data[...] + other_data[...])
    interface[...] = -y
    parent_data[...] = outer_data[...] + dot3(outward[...], y)


def local(kernel, outs, flops, *args):
    moved = sum(a.size * a.dtype.itemsize for a in args)
    return pl.pallas_call(
        kernel,
        out_shape=[jax.ShapeDtypeStruct(s, jnp.float32) for s in outs],
        in_specs=[VMEM] * len(args),
        out_specs=[VMEM] * len(outs),
        compiler_params=pltpu.CompilerParams(vmem_limit_bytes=32 * 1024 * 1024),
        cost_estimate=pl.CostEstimate(flops=flops, bytes_accessed=moved, transcendentals=0),
    )(*args)


def from_partner(block, axis, stride):
    count = lax.axis_size(axis)
    route = []
    for low in range(count):
        high = low | 1 << stride
        if high != low and high < count:
            route += [(low, high), (high, low)]
    return lax.ppermute(block, axis, route)


def front_kernel(*refs):
    far, near = refs[:5], refs[8:13]
    parent, neumann, other_parent = refs[5:8]
    flow_x, part, ends, low_halo, high_halo, source, send_sem, receive_sem, load_sem = refs[13:]
    velocity, field, conductivity, wall_flags, solution_map = near
    loads = [pltpu.make_async_copy(far[i], near[i], load_sem.at[i]) for i in range(5)]
    for i in (1, 2, 3, 0, 4):
        loads[i].start()
    slab = lax.axis_index("slab")
    count = lax.axis_size("slab")
    has_low, has_high = slab > 0, slab < count - 1
    lower = lax.max(slab - 1, 0)
    upper = lax.min(slab + 1, count - 1)
    box = lax.axis_index("box")
    across_box = box + 2 - 4 * lax.rem(lax.div(box, 2), 2)
    barrier = pltpu.get_barrier_semaphore()
    pl.semaphore_signal(barrier, inc=1, device_id={"box": across_box}, device_id_type=MESH)

    @pl.when(has_low)
    def _():
        pl.semaphore_signal(barrier, inc=1, device_id={"slab": lower}, device_id_type=MESH)

    @pl.when(has_high)
    def _():
        pl.semaphore_signal(barrier, inc=1, device_id={"slab": upper}, device_id_type=MESH)

    sizex, sizey, depth, snaps = part.shape
    plane = (sizey, depth, snaps)
    at_z = lax.broadcasted_iota(jnp.int32, plane, 1)
    first, last = at_z == 0, at_z == depth - 1
    none = jnp.zeros((1, depth, snaps), jnp.float32)
    flow_x[0] = jnp.zeros(plane, jnp.float32)
    flow_x[sizex + 1] = jnp.zeros(plane, jnp.float32)

    def moved(a, steps):
        flat = pltpu.roll(a.reshape(sizey * depth, snaps), steps, 0)
        return flat.reshape(plane)

    def current(x, carry):
        sigma = conductivity[x] * jnp.where(wall_flags[x] == 1, WALL_RATIO, 1.0)
        m0, m1, m2 = [
            jnp.broadcast_to((sigma * field[d, x])[:, :, None], plane) for d in range(3)
        ]
        v0, v1, v2 = [velocity[d, x].astype(jnp.float32) for d in range(3)]
        flow_x[x + 1] = v1 * m2 - v2 * m1
        flow_y = v2 * m0 - v0 * m2
        flow_z = v0 * m1 - v1 * m0
        ends[0, x] = jnp.sum(jnp.where(first, flow_z, 0.0), axis=1, keepdims=True)
        ends[1, x] = jnp.sum(jnp.where(last, flow_z, 0.0), axis=1, keepdims=True)
        after = jnp.where(last, 0.0, moved(flow_z, sizey * depth - 1))
        before = jnp.where(first, 0.0, moved(flow_z, 1))
        across = jnp.concatenate([flow_y[1:], none]) - jnp.concatenate([none, flow_y[:-1]])
        part[x] = across + (after - before)
        return carry

    for i in range(4):
        loads[i].wait()
    lax.fori_loop(0, sizex, current, 0)
    pl.semaphore_wait(barrier, 1 + has_low.astype(jnp.int32) + has_high.astype(jnp.int32))
    down = pltpu.make_async_remote_copy(
        src_ref=ends.at[0],
        dst_ref=high_halo,
        send_sem=send_sem.at[0],
        recv_sem=receive_sem.at[0],
        device_id={"slab": lower},
        device_id_type=MESH,
    )
    up = pltpu.make_async_remote_copy(
        src_ref=ends.at[1],
        dst_ref=low_halo,
        send_sem=send_sem.at[1],
        recv_sem=receive_sem.at[1],
        device_id={"slab": upper},
        device_id_type=MESH,
    )

    swap = pltpu.make_async_remote_copy(
        src_ref=parent,
        dst_ref=other_parent,
        send_sem=send_sem.at[2],
        recv_sem=receive_sem.at[2],
        device_id={"box": across_box},
        device_id_type=MESH,
    )

    @pl.when(has_low)
    def _():
        down.start()

    @pl.when(jnp.logical_not(has_low))
    def _():
        low_halo[...] = jnp.zeros_like(low_halo)

    @pl.when(has_high)
    def _():
        up.start()

    @pl.when(jnp.logical_not(has_high))
    def _():
        high_halo[...] = jnp.zeros_like(high_halo)

    swap.start()

    def along(x, carry):
        part[x] += flow_x[x + 2] - flow_x[x]
        return carry

    lax.fori_loop(0, sizex, along, 0)

    @pl.when(has_low)
    def _():
        up.wait_recv()
        down.wait_send()

    @pl.when(has_high)
    def _():
        down.wait_recv()
        up.wait_send()

    def finish(x, carry):
        low = jnp.broadcast_to(low_halo[x], plane)
        high = jnp.broadcast_to(high_halo[x], plane)
        ending = jnp.where(last, high, 0.0) - jnp.where(first, low, 0.0)
        rows = sizey * depth
        whole = (0.5 * (part[x] + ending)).reshape(rows, snaps)
        source[pl.ds(pl.multiple_of(x * rows, rows), rows), :] = whole.astype(jnp.bfloat16)
        return carry

    lax.fori_loop(0, sizex, finish, 0)
    loads[4].wait()
    neumann[...] = jnp.dot(solution_map[...], source[...], preferred_element_type=jnp.float32)
    swap.wait()


def front(velocity, field, conductivity, wall_flags, solution_map, parent):
    arrays = (velocity, field, conductivity, wall_flags, solution_map)
    _, sizex, sizey, depth, snaps = velocity.shape
    f32 = jnp.float32
    return pl.pallas_call(
        front_kernel,
        out_shape=[
            jax.ShapeDtypeStruct((solution_map.shape[0], snaps), f32),
            jax.ShapeDtypeStruct(parent.shape, f32),
        ],
        in_specs=[pl.BlockSpec(memory_space=pltpu.MemorySpace.HBM)] * 5 + [VMEM],
        out_specs=[VMEM] * 2,
        scratch_shapes=[pltpu.VMEM(a.shape, a.dtype) for a in arrays]
        + [
            pltpu.VMEM((sizex + 2, sizey, depth, snaps), f32),
            pltpu.VMEM((sizex, sizey, depth, snaps), f32),
            pltpu.VMEM((2, sizex, sizey, 1, snaps), f32),
            pltpu.VMEM((sizex, sizey, 1, snaps), f32),
            pltpu.VMEM((sizex, sizey, 1, snaps), f32),
            pltpu.VMEM((sizex * sizey * depth, snaps), jnp.bfloat16),
            pltpu.SemaphoreType.DMA((3,)),
            pltpu.SemaphoreType.DMA((3,)),
            pltpu.SemaphoreType.DMA((5,)),
        ],
        compiler_params=pltpu.CompilerParams(
            collective_id=0, has_side_effects=True, vmem_limit_bytes=40 * 1024 * 1024
        ),
        cost_estimate=pl.CostEstimate(
            flops=2 * solution_map.size * snaps, bytes_accessed=4 * 2**20, transcendentals=0
        ),
    )(*arrays, parent)


def on_device(velocity, field, conductivity, wall_flags, leaf_solution, leaf_dtn):
    dtn_map = leaf_dtn[0, 0]
    width = dtn_map.shape[0] // 2
    square = (width, width)
    other_map = from_partner(dtn_map, "box", 0)
    cube = 2 * width**3
    schur, inverse, parent, outward = local(
        map_kernel, [square] * 4, 30 * cube, dtn_map, other_map
    )
    neumann, other_parent = front(
        velocity[0], field[0], conductivity[0], wall_flags[0], leaf_solution[0, 0], parent
    )
    thin = (width, neumann.shape[1])
    other_neumann = from_partner(neumann, "box", 0)
    schur_two, inverse_two = local(
        second_map_kernel, [square] * 2, 20 * cube, parent, other_parent
    )
    inner_data, outer_data = local(
        data_kernel, [thin] * 2, 6 * cube, dtn_map, other_map, neumann, other_neumann, schur, inverse
    )
    other_inner = from_partner(inner_data, "box", 1)
    interface, own_side = local(
        second_data_kernel,
        [thin] * 2,
        4 * cube,
        inner_data,
        other_inner,
        schur_two,
        inverse_two,
        outward,
        outer_data,
    )
    other_side = from_partner(own_side, "box", 1)
    left = lax.axis_index("box") >> 1 & 1 == 0
    first = jnp.where(left, own_side, other_side)
    second = jnp.where(left, other_side, own_side)
    return (interface[None, None], jnp.concatenate([first, second], axis=0)[None, None])


def solution(mesh):
    return jax.shard_map(
        on_device,
        mesh=mesh,
        in_specs=(
            P("box", None, None, None, "slab", None),
            P("box", None, None, None, "slab"),
            P("box", None, None, "slab"),
            P("box", None, None, "slab"),
            P("box", "slab", None, None),
            P("box", "slab", None, None),
        ),
        out_specs=(P("box", "slab", None, None), P("box", "slab", None, None)),
        check_vma=False,
    )
```

```python
import functools

import jax
import jax.numpy as jnp
from jax import lax
from jax.experimental import pallas as pl
from jax.experimental.pallas import tpu as pltpu
from jax.sharding import PartitionSpec as P

WALL_RATIO = 8.0
SQUARINGS = 3
NEWTON_LIMIT = 12
CLOSE = 0.05
MESH = pl.DeviceIdType.MESH
VMEM = pl.BlockSpec(memory_space=pltpu.VMEM)


def dot1(a, b):
    return jnp.dot(
        a.astype(jnp.bfloat16), b.astype(jnp.bfloat16), preferred_element_type=jnp.float32
    )


def halves(a):
    high = a.astype(jnp.bfloat16)
    return high, (a - high.astype(jnp.float32)).astype(jnp.bfloat16)


def dot3(a, b):
    ah, al = halves(a)
    bh, bl = halves(b)
    return dot1(ah, bh) + (dot1(ah, bl) + dot1(al, bh))


def eye(width):
    rows = lax.broadcasted_iota(jnp.int32, (width, width), 0)
    columns = lax.broadcasted_iota(jnp.int32, (width, width), 1)
    return (rows == columns).astype(jnp.float32)


def approximate_inverse(schur, inverse):
    width = schur.shape[0]
    unit = eye(width)
    matrix = schur[...]
    scale = jnp.sum(unit * matrix) / jnp.sum(matrix * matrix)
    power = unit - scale * matrix
    total = unit + power
    for _ in range(SQUARINGS):
        power = dot1(power, power)
        total = total + dot1(total, power)
    inverse[...] = scale * total

    def error():
        return unit - dot3(schur[...], inverse[...])

    first = error()

    def body(state):
        step, residual, norm = state
        inverse[...] += dot3(inverse[...], residual)
        residual = error()
        return step + 1, residual, jnp.sum(residual * residual)

    def far(state):
        step, residual, norm = state
        return jnp.logical_and(step < NEWTON_LIMIT, jnp.logical_not(norm < CLOSE * CLOSE))

    step, residual, norm = lax.while_loop(far, body, (0, first, jnp.sum(first * first)))
    good = norm < CLOSE * CLOSE

    @pl.when(good)
    def _():
        inverse[...] += dot1(inverse[...], residual)

    @pl.when(jnp.logical_not(good))
    def _():
        inverse[...] = schur[...]
        lane = lax.broadcasted_iota(jnp.int32, (width, width), 1)
        sublane = lax.broadcasted_iota(jnp.int32, (width, width), 0)

        def eliminate(k, carry):
            m = inverse[...]
            at = lane == k
            row = jnp.sum(jnp.where(sublane == k, m, 0.0), axis=0, keepdims=True)
            column = jnp.sum(jnp.where(at, m, 0.0), axis=1, keepdims=True)
            at_row = lax.broadcasted_iota(jnp.int32, (1, width), 1) == k
            pivot = jnp.sum(jnp.where(at_row, row, 0.0), axis=1, keepdims=True)
            scaled = jnp.where(at_row, 1.0, row) / pivot
            inverse[...] = jnp.where(sublane == k, scaled, jnp.where(at, 0.0, m) - column * scaled)
            return carry

        lax.fori_loop(0, width, eliminate, 0)


def solve(schur, inverse, b):
    y = dot1(inverse, b)
    return y + dot1(inverse, b - dot3(schur, y))


def roles():
    box = lax.axis_index("box")
    low, high = lax.rem(box, 2), lax.rem(lax.div(box, 2), 2)
    return low, low != high


def block(ref, row, column):
    width = ref.shape[0] // 2
    r = pl.multiple_of(row * width, width)
    c = pl.multiple_of(column * width, width)
    return ref[pl.ds(r, width), pl.ds(c, width)]


def face(ref, at):
    width = ref.shape[0] // 2
    return ref[pl.ds(pl.multiple_of(at * width, width), width), :]


def map_kernel(own, other, schur, inverse, parent, outward):
    low, inner = roles()
    mine, theirs = 1 - low, low
    schur[...] = block(own, mine, mine) + block(other, theirs, theirs)
    approximate_inverse(schur, inverse)
    inner_mi = jnp.where(inner, block(own, mine, low), block(other, theirs, mine))
    inner_im = jnp.where(inner, block(own, low, mine), block(other, mine, theirs))
    inner_ii = jnp.where(inner, block(own, low, low), block(other, mine, mine))
    outer_om = jnp.where(inner, block(other, mine, theirs), block(own, low, mine))
    weights = solve(schur[...], inverse[...], inner_mi)
    parent[...] = inner_ii - dot3(inner_im, weights)
    outward[...] = dot3(outer_om, weights)


def data_kernel(own, other, data, other_data, schur, inverse, inner_data, outer_data):
    low, inner = roles()
    mine, theirs = 1 - low, low
    b = face(data, mine) + face(other_data, theirs)
    interface = solve(schur[...], inverse[...], b)
    inner_im = jnp.where(inner, block(own, low, mine), block(other, mine, theirs))
    outer_om = jnp.where(inner, block(other, mine, theirs), block(own, low, mine))
    a, c = face(data, low), face(other_data, mine)
    inner_data[...] = jnp.where(inner, a, c) - dot3(inner_im, interface)
    outer_data[...] = jnp.where(inner, c, a) - dot3(outer_om, interface)


def second_map_kernel(parent, other_parent, schur, inverse):
    schur[...] = parent[...] + other_parent[...]
    approximate_inverse(schur, inverse)


def second_data_kernel(data, other_data, schur, inverse, outward, outer_data, interface, parent_data):
    y = solve(schur[...], inverse[...], data[...] + other_data[...])
    interface[...] = -y
    parent_data[...] = outer_data[...] + dot3(outward[...], y)


def local(kernel, outs, flops, *args):
    moved = sum(a.size * a.dtype.itemsize for a in args)
    return pl.pallas_call(
        kernel,
        out_shape=[jax.ShapeDtypeStruct(s, jnp.float32) for s in outs],
        in_specs=[VMEM] * len(args),
        out_specs=[VMEM] * len(outs),
        compiler_params=pltpu.CompilerParams(vmem_limit_bytes=32 * 1024 * 1024),
        cost_estimate=pl.CostEstimate(flops=flops, bytes_accessed=moved, transcendentals=0),
    )(*args)


def from_partner(block, axis, stride):
    count = lax.axis_size(axis)
    route = []
    for low in range(count):
        high = low | 1 << stride
        if high != low and high < count:
            route += [(low, high), (high, low)]
    return lax.ppermute(block, axis, route)


def front_kernel(*refs):
    far, near = refs[:5], refs[8:13]
    parent, neumann, other_parent = refs[5:8]
    flow_x, part, ends, low_halo, high_halo, source, send_sem, receive_sem, load_sem = refs[13:]
    velocity, field, conductivity, wall_flags, solution_map = near
    loads = [pltpu.make_async_copy(far[i], near[i], load_sem.at[i]) for i in range(5)]
    for i in (1, 2, 3, 0, 4):
        loads[i].start()
    slab = lax.axis_index("slab")
    count = lax.axis_size("slab")
    has_low, has_high = slab > 0, slab < count - 1
    lower = lax.max(slab - 1, 0)
    upper = lax.min(slab + 1, count - 1)
    box = lax.axis_index("box")
    across_box = box + 2 - 4 * lax.rem(lax.div(box, 2), 2)
    barrier = pltpu.get_barrier_semaphore()
    pl.semaphore_signal(barrier, inc=1, device_id={"box": across_box}, device_id_type=MESH)

    @pl.when(has_low)
    def _():
        pl.semaphore_signal(barrier, inc=1, device_id={"slab": lower}, device_id_type=MESH)

    @pl.when(has_high)
    def _():
        pl.semaphore_signal(barrier, inc=1, device_id={"slab": upper}, device_id_type=MESH)

    pl.semaphore_wait(barrier, 1 + has_low.astype(jnp.int32) + has_high.astype(jnp.int32))
    swap = pltpu.make_async_remote_copy(
        src_ref=parent,
        dst_ref=other_parent,
        send_sem=send_sem.at[2],
        recv_sem=receive_sem.at[2],
        device_id={"box": across_box},
        device_id_type=MESH,
    )
    swap.start()
    sizex, sizey, depth, snaps = part.shape
    plane = (sizey, depth, snaps)
    at_z = lax.broadcasted_iota(jnp.int32, plane, 1)
    first, last = at_z == 0, at_z == depth - 1
    none = jnp.zeros((1, depth, snaps), jnp.float32)
    flow_x[0] = jnp.zeros(plane, jnp.float32)
    flow_x[sizex + 1] = jnp.zeros(plane, jnp.float32)

    def moved(a, steps):
        flat = pltpu.roll(a.reshape(sizey * depth, snaps), steps, 0)
        return flat.reshape(plane)

    def current(x, carry):
        sigma = conductivity[x] * jnp.where(wall_flags[x] == 1, WALL_RATIO, 1.0)
        m0, m1, m2 = [
            jnp.broadcast_to((sigma * field[d, x])[:, :, None], plane) for d in range(3)
        ]
        v0, v1, v2 = [velocity[d, x].astype(jnp.float32) for d in range(3)]
        flow_x[x + 1] = v1 * m2 - v2 * m1
        flow_y = v2 * m0 - v0 * m2
        flow_z = v0 * m1 - v1 * m0
        ends[0, x] = jnp.sum(jnp.where(first, flow_z, 0.0), axis=1, keepdims=True)
        ends[1, x] = jnp.sum(jnp.where(last, flow_z, 0.0), axis=1, keepdims=True)
        after = jnp.where(last, 0.0, moved(flow_z, sizey * depth - 1))
        before = jnp.where(first, 0.0, moved(flow_z, 1))
        across = jnp.concatenate([flow_y[1:], none]) - jnp.concatenate([none, flow_y[:-1]])
        part[x] = across + (after - before)
        return carry

    for i in range(4):
        loads[i].wait()
    lax.fori_loop(0, sizex, current, 0)
    down = pltpu.make_async_remote_copy(
        src_ref=ends.at[0],
        dst_ref=high_halo,
        send_sem=send_sem.at[0],
        recv_sem=receive_sem.at[0],
        device_id={"slab": lower},
        device_id_type=MESH,
    )
    up = pltpu.make_async_remote_copy(
        src_ref=ends.at[1],
        dst_ref=low_halo,
        send_sem=send_sem.at[1],
        recv_sem=receive_sem.at[1],
        device_id={"slab": upper},
        device_id_type=MESH,
    )

    @pl.when(has_low)
    def _():
        down.start()

    @pl.when(jnp.logical_not(has_low))
    def _():
        low_halo[...] = jnp.zeros_like(low_halo)

    @pl.when(has_high)
    def _():
        up.start()

    @pl.when(jnp.logical_not(has_high))
    def _():
        high_halo[...] = jnp.zeros_like(high_halo)

    def along(x, carry):
        part[x] += flow_x[x + 2] - flow_x[x]
        return carry

    lax.fori_loop(0, sizex, along, 0)

    @pl.when(has_low)
    def _():
        up.wait_recv()
        down.wait_send()

    @pl.when(has_high)
    def _():
        down.wait_recv()
        up.wait_send()

    def finish(x, carry):
        low = jnp.broadcast_to(low_halo[x], plane)
        high = jnp.broadcast_to(high_halo[x], plane)
        ending = jnp.where(last, high, 0.0) - jnp.where(first, low, 0.0)
        rows = sizey * depth
        whole = (0.5 * (part[x] + ending)).reshape(rows, snaps)
        source[pl.ds(pl.multiple_of(x * rows, rows), rows), :] = whole.astype(jnp.bfloat16)
        return carry

    lax.fori_loop(0, sizex, finish, 0)
    loads[4].wait()
    neumann[...] = jnp.dot(solution_map[...], source[...], preferred_element_type=jnp.float32)
    swap.wait()


def front(velocity, field, conductivity, wall_flags, solution_map, parent):
    arrays = (velocity, field, conductivity, wall_flags, solution_map)
    _, sizex, sizey, depth, snaps = velocity.shape
    f32 = jnp.float32
    return pl.pallas_call(
        front_kernel,
        out_shape=[
            jax.ShapeDtypeStruct((solution_map.shape[0], snaps), f32),
            jax.ShapeDtypeStruct(parent.shape, f32),
        ],
        in_specs=[pl.BlockSpec(memory_space=pltpu.MemorySpace.HBM)] * 5 + [VMEM],
        out_specs=[VMEM] * 2,
        scratch_shapes=[pltpu.VMEM(a.shape, a.dtype) for a in arrays]
        + [
            pltpu.VMEM((sizex + 2, sizey, depth, snaps), f32),
            pltpu.VMEM((sizex, sizey, depth, snaps), f32),
            pltpu.VMEM((2, sizex, sizey, 1, snaps), f32),
            pltpu.VMEM((sizex, sizey, 1, snaps), f32),
            pltpu.VMEM((sizex, sizey, 1, snaps), f32),
            pltpu.VMEM((sizex * sizey * depth, snaps), jnp.bfloat16),
            pltpu.SemaphoreType.DMA((3,)),
            pltpu.SemaphoreType.DMA((3,)),
            pltpu.SemaphoreType.DMA((5,)),
        ],
        compiler_params=pltpu.CompilerParams(
            collective_id=0, has_side_effects=True, vmem_limit_bytes=40 * 1024 * 1024
        ),
        cost_estimate=pl.CostEstimate(
            flops=2 * solution_map.size * snaps, bytes_accessed=4 * 2**20, transcendentals=0
        ),
    )(*arrays, parent)


def on_device(velocity, field, conductivity, wall_flags, leaf_solution, leaf_dtn):
    dtn_map = leaf_dtn[0, 0]
    width = dtn_map.shape[0] // 2
    square = (width, width)
    other_map = from_partner(dtn_map, "box", 0)
    cube = 2 * width**3
    schur, inverse, parent, outward = local(
        map_kernel, [square] * 4, 30 * cube, dtn_map, other_map
    )
    neumann, other_parent = front(
        velocity[0], field[0], conductivity[0], wall_flags[0], leaf_solution[0, 0], parent
    )
    thin = (width, neumann.shape[1])
    other_neumann = from_partner(neumann, "box", 0)
    schur_two, inverse_two = local(
        second_map_kernel, [square] * 2, 20 * cube, parent, other_parent
    )
    inner_data, outer_data = local(
        data_kernel, [thin] * 2, 6 * cube, dtn_map, other_map, neumann, other_neumann, schur, inverse
    )
    other_inner = from_partner(inner_data, "box", 1)
    interface, own_side = local(
        second_data_kernel,
        [thin] * 2,
        4 * cube,
        inner_data,
        other_inner,
        schur_two,
        inverse_two,
        outward,
        outer_data,
    )
    other_side = from_partner(own_side, "box", 1)
    left = lax.axis_index("box") >> 1 & 1 == 0
    first = jnp.where(left, own_side, other_side)
    second = jnp.where(left, other_side, own_side)
    return (interface[None, None], jnp.concatenate([first, second], axis=0)[None, None])


def solution(mesh):
    return jax.shard_map(
        on_device,
        mesh=mesh,
        in_specs=(
            P("box", None, None, None, "slab", None),
            P("box", None, None, None, "slab"),
            P("box", None, None, "slab"),
            P("box", None, None, "slab"),
            P("box", "slab", None, None),
            P("box", "slab", None, None),
        ),
        out_specs=(P("box", "slab", None, None), P("box", "slab", None, None)),
        check_vma=False,
    )
```

```python
import functools

import jax
import jax.numpy as jnp
from jax import lax
from jax.experimental import pallas as pl
from jax.experimental.pallas import tpu as pltpu
from jax.sharding import PartitionSpec as P

WALL_RATIO = 8.0
SQUARINGS = 3
NEWTON_LIMIT = 12
CLOSE = 0.05
MESH = pl.DeviceIdType.MESH
VMEM = pl.BlockSpec(memory_space=pltpu.VMEM)


def dot1(a, b):
    return jnp.dot(
        a.astype(jnp.bfloat16), b.astype(jnp.bfloat16), preferred_element_type=jnp.float32
    )


def halves(a):
    high = a.astype(jnp.bfloat16)
    return high, (a - high.astype(jnp.float32)).astype(jnp.bfloat16)


def dot3(a, b):
    ah, al = halves(a)
    bh, bl = halves(b)
    return dot1(ah, bh) + (dot1(ah, bl) + dot1(al, bh))


def eye(width):
    rows = lax.broadcasted_iota(jnp.int32, (width, width), 0)
    columns = lax.broadcasted_iota(jnp.int32, (width, width), 1)
    return (rows == columns).astype(jnp.float32)


def approximate_inverse(schur, inverse):
    width = schur.shape[0]
    unit = eye(width)
    matrix = schur[...]
    scale = jnp.sum(unit * matrix) / jnp.sum(matrix * matrix)
    power = unit - scale * matrix
    total = unit + power
    for _ in range(SQUARINGS):
        power = dot1(power, power)
        total = total + dot1(total, power)
    inverse[...] = scale * total

    def error():
        return unit - dot3(schur[...], inverse[...])

    first = error()

    def body(state):
        step, residual, norm = state
        inverse[...] += dot3(inverse[...], residual)
        residual = error()
        return step + 1, residual, jnp.sum(residual * residual)

    def far(state):
        step, residual, norm = state
        return jnp.logical_and(step < NEWTON_LIMIT, jnp.logical_not(norm < CLOSE * CLOSE))

    step, residual, norm = lax.while_loop(far, body, (0, first, jnp.sum(first * first)))
    good = norm < CLOSE * CLOSE

    @pl.when(good)
    def _():
        inverse[...] += dot1(inverse[...], residual)

    @pl.when(jnp.logical_not(good))
    def _():
        inverse[...] = schur[...]
        lane = lax.broadcasted_iota(jnp.int32, (width, width), 1)
        sublane = lax.broadcasted_iota(jnp.int32, (width, width), 0)

        def eliminate(k, carry):
            m = inverse[...]
            at = lane == k
            row = jnp.sum(jnp.where(sublane == k, m, 0.0), axis=0, keepdims=True)
            column = jnp.sum(jnp.where(at, m, 0.0), axis=1, keepdims=True)
            at_row = lax.broadcasted_iota(jnp.int32, (1, width), 1) == k
            pivot = jnp.sum(jnp.where(at_row, row, 0.0), axis=1, keepdims=True)
            scaled = jnp.where(at_row, 1.0, row) / pivot
            inverse[...] = jnp.where(sublane == k, scaled, jnp.where(at, 0.0, m) - column * scaled)
            return carry

        lax.fori_loop(0, width, eliminate, 0)


def solve(schur, inverse, b):
    y = dot1(inverse, b)
    return y + dot1(inverse, b - dot3(schur, y))


def roles():
    box = lax.axis_index("box")
    low, high = lax.rem(box, 2), lax.rem(lax.div(box, 2), 2)
    return low, low != high


def block(ref, row, column):
    width = ref.shape[0] // 2
    r = pl.multiple_of(row * width, width)
    c = pl.multiple_of(column * width, width)
    return ref[pl.ds(r, width), pl.ds(c, width)]


def face(ref, at):
    width = ref.shape[0] // 2
    return ref[pl.ds(pl.multiple_of(at * width, width), width), :]


def map_kernel(own, other, schur, inverse, parent, outward):
    low, inner = roles()
    mine, theirs = 1 - low, low
    schur[...] = block(own, mine, mine) + block(other, theirs, theirs)
    approximate_inverse(schur, inverse)
    inner_mi = jnp.where(inner, block(own, mine, low), block(other, theirs, mine))
    inner_im = jnp.where(inner, block(own, low, mine), block(other, mine, theirs))
    inner_ii = jnp.where(inner, block(own, low, low), block(other, mine, mine))
    outer_om = jnp.where(inner, block(other, mine, theirs), block(own, low, mine))
    weights = solve(schur[...], inverse[...], inner_mi)
    parent[...] = inner_ii - dot3(inner_im, weights)
    outward[...] = dot3(outer_om, weights)


def data_kernel(own, other, data, other_data, schur, inverse, inner_data, outer_data):
    low, inner = roles()
    mine, theirs = 1 - low, low
    b = face(data, mine) + face(other_data, theirs)
    interface = solve(schur[...], inverse[...], b)
    inner_im = jnp.where(inner, block(own, low, mine), block(other, mine, theirs))
    outer_om = jnp.where(inner, block(other, mine, theirs), block(own, low, mine))
    a, c = face(data, low), face(other_data, mine)
    inner_data[...] = jnp.where(inner, a, c) - dot3(inner_im, interface)
    outer_data[...] = jnp.where(inner, c, a) - dot3(outer_om, interface)


def second_map_kernel(parent, other_parent, schur, inverse):
    schur[...] = parent[...] + other_parent[...]
    approximate_inverse(schur, inverse)


def second_data_kernel(data, other_data, schur, inverse, outward, outer_data, interface, parent_data):
    y = solve(schur[...], inverse[...], data[...] + other_data[...])
    interface[...] = -y
    parent_data[...] = outer_data[...] + dot3(outward[...], y)


def local(kernel, outs, flops, *args):
    moved = sum(a.size * a.dtype.itemsize for a in args)
    return pl.pallas_call(
        kernel,
        out_shape=[jax.ShapeDtypeStruct(s, jnp.float32) for s in outs],
        in_specs=[VMEM] * len(args),
        out_specs=[VMEM] * len(outs),
        compiler_params=pltpu.CompilerParams(vmem_limit_bytes=32 * 1024 * 1024),
        cost_estimate=pl.CostEstimate(flops=flops, bytes_accessed=moved, transcendentals=0),
    )(*args)


def from_partner(block, axis, stride):
    count = lax.axis_size(axis)
    route = []
    for low in range(count):
        high = low | 1 << stride
        if high != low and high < count:
            route += [(low, high), (high, low)]
    return lax.ppermute(block, axis, route)


def front_kernel(*refs):
    far, near = refs[:5], refs[8:13]
    parent, neumann, other_parent = refs[5:8]
    flow_x, part, ends, low_halo, high_halo, source, send_sem, receive_sem, load_sem = refs[13:]
    velocity, field, conductivity, wall_flags, solution_map = near
    loads = [pltpu.make_async_copy(far[i], near[i], load_sem.at[i]) for i in range(5)]
    for i in (1, 2, 3, 0, 4):
        loads[i].start()
    slab = lax.axis_index("slab")
    count = lax.axis_size("slab")
    has_low, has_high = slab > 0, slab < count - 1
    lower = lax.max(slab - 1, 0)
    upper = lax.min(slab + 1, count - 1)
    box = lax.axis_index("box")
    across_box = box + 2 - 4 * lax.rem(lax.div(box, 2), 2)
    barrier = pltpu.get_barrier_semaphore()
    core = lax.rem(box, 2)
    beside = box + 1 - 2 * core
    share = parent.shape[0] // 2
    mine = pl.ds(pl.multiple_of(core * share, share), share)
    pl.semaphore_signal(barrier, inc=1, device_id={"box": across_box}, device_id_type=MESH)
    pl.semaphore_signal(barrier, inc=1, device_id={"box": beside}, device_id_type=MESH)

    @pl.when(has_low)
    def _():
        pl.semaphore_signal(barrier, inc=1, device_id={"slab": lower}, device_id_type=MESH)

    @pl.when(has_high)
    def _():
        pl.semaphore_signal(barrier, inc=1, device_id={"slab": upper}, device_id_type=MESH)

    pl.semaphore_wait(barrier, 2 + has_low.astype(jnp.int32) + has_high.astype(jnp.int32))
    swap = pltpu.make_async_remote_copy(
        src_ref=parent.at[mine],
        dst_ref=other_parent.at[mine],
        send_sem=send_sem.at[2],
        recv_sem=receive_sem.at[2],
        device_id={"box": across_box},
        device_id_type=MESH,
    )
    swap.start()
    sizex, sizey, depth, snaps = part.shape
    plane = (sizey, depth, snaps)
    at_z = lax.broadcasted_iota(jnp.int32, plane, 1)
    first, last = at_z == 0, at_z == depth - 1
    none = jnp.zeros((1, depth, snaps), jnp.float32)
    flow_x[0] = jnp.zeros(plane, jnp.float32)
    flow_x[sizex + 1] = jnp.zeros(plane, jnp.float32)

    def moved(a, steps):
        flat = pltpu.roll(a.reshape(sizey * depth, snaps), steps, 0)
        return flat.reshape(plane)

    def current(x, carry):
        sigma = conductivity[x] * jnp.where(wall_flags[x] == 1, WALL_RATIO, 1.0)
        m0, m1, m2 = [
            jnp.broadcast_to((sigma * field[d, x])[:, :, None], plane) for d in range(3)
        ]
        v0, v1, v2 = [velocity[d, x].astype(jnp.float32) for d in range(3)]
        flow_x[x + 1] = v1 * m2 - v2 * m1
        flow_y = v2 * m0 - v0 * m2
        flow_z = v0 * m1 - v1 * m0
        ends[0, x] = jnp.sum(jnp.where(first, flow_z, 0.0), axis=1, keepdims=True)
        ends[1, x] = jnp.sum(jnp.where(last, flow_z, 0.0), axis=1, keepdims=True)
        after = jnp.where(last, 0.0, moved(flow_z, sizey * depth - 1))
        before = jnp.where(first, 0.0, moved(flow_z, 1))
        across = jnp.concatenate([flow_y[1:], none]) - jnp.concatenate([none, flow_y[:-1]])
        part[x] = across + (after - before)
        return carry

    for i in range(4):
        loads[i].wait()
    lax.fori_loop(0, sizex, current, 0)
    down = pltpu.make_async_remote_copy(
        src_ref=ends.at[0],
        dst_ref=high_halo,
        send_sem=send_sem.at[0],
        recv_sem=receive_sem.at[0],
        device_id={"slab": lower},
        device_id_type=MESH,
    )
    up = pltpu.make_async_remote_copy(
        src_ref=ends.at[1],
        dst_ref=low_halo,
        send_sem=send_sem.at[1],
        recv_sem=receive_sem.at[1],
        device_id={"slab": upper},
        device_id_type=MESH,
    )

    @pl.when(has_low)
    def _():
        down.start()

    @pl.when(jnp.logical_not(has_low))
    def _():
        low_halo[...] = jnp.zeros_like(low_halo)

    @pl.when(has_high)
    def _():
        up.start()

    @pl.when(jnp.logical_not(has_high))
    def _():
        high_halo[...] = jnp.zeros_like(high_halo)

    def along(x, carry):
        part[x] += flow_x[x + 2] - flow_x[x]
        return carry

    lax.fori_loop(0, sizex, along, 0)

    @pl.when(has_low)
    def _():
        up.wait_recv()
        down.wait_send()

    @pl.when(has_high)
    def _():
        down.wait_recv()
        up.wait_send()

    def finish(x, carry):
        low = jnp.broadcast_to(low_halo[x], plane)
        high = jnp.broadcast_to(high_halo[x], plane)
        ending = jnp.where(last, high, 0.0) - jnp.where(first, low, 0.0)
        rows = sizey * depth
        whole = (0.5 * (part[x] + ending)).reshape(rows, snaps)
        source[pl.ds(pl.multiple_of(x * rows, rows), rows), :] = whole.astype(jnp.bfloat16)
        return carry

    lax.fori_loop(0, sizex, finish, 0)
    swap.wait()
    relay = pltpu.make_async_remote_copy(
        src_ref=other_parent.at[mine],
        dst_ref=other_parent.at[mine],
        send_sem=send_sem.at[3],
        recv_sem=receive_sem.at[3],
        device_id={"box": beside},
        device_id_type=MESH,
    )
    relay.start()
    loads[4].wait()
    neumann[...] = jnp.dot(solution_map[...], source[...], preferred_element_type=jnp.float32)
    relay.wait()


def front(velocity, field, conductivity, wall_flags, solution_map, parent):
    arrays = (velocity, field, conductivity, wall_flags, solution_map)
    _, sizex, sizey, depth, snaps = velocity.shape
    f32 = jnp.float32
    return pl.pallas_call(
        front_kernel,
        out_shape=[
            jax.ShapeDtypeStruct((solution_map.shape[0], snaps), f32),
            jax.ShapeDtypeStruct(parent.shape, f32),
        ],
        in_specs=[pl.BlockSpec(memory_space=pltpu.MemorySpace.HBM)] * 5 + [VMEM],
        out_specs=[VMEM] * 2,
        scratch_shapes=[pltpu.VMEM(a.shape, a.dtype) for a in arrays]
        + [
            pltpu.VMEM((sizex + 2, sizey, depth, snaps), f32),
            pltpu.VMEM((sizex, sizey, depth, snaps), f32),
            pltpu.VMEM((2, sizex, sizey, 1, snaps), f32),
            pltpu.VMEM((sizex, sizey, 1, snaps), f32),
            pltpu.VMEM((sizex, sizey, 1, snaps), f32),
            pltpu.VMEM((sizex * sizey * depth, snaps), jnp.bfloat16),
            pltpu.SemaphoreType.DMA((4,)),
            pltpu.SemaphoreType.DMA((4,)),
            pltpu.SemaphoreType.DMA((5,)),
        ],
        compiler_params=pltpu.CompilerParams(
            collective_id=0, has_side_effects=True, vmem_limit_bytes=40 * 1024 * 1024
        ),
        cost_estimate=pl.CostEstimate(
            flops=2 * solution_map.size * snaps, bytes_accessed=4 * 2**20, transcendentals=0
        ),
    )(*arrays, parent)


def on_device(velocity, field, conductivity, wall_flags, leaf_solution, leaf_dtn):
    dtn_map = leaf_dtn[0, 0]
    width = dtn_map.shape[0] // 2
    square = (width, width)
    other_map = from_partner(dtn_map, "box", 0)
    cube = 2 * width**3
    schur, inverse, parent, outward = local(
        map_kernel, [square] * 4, 30 * cube, dtn_map, other_map
    )
    neumann, other_parent = front(
        velocity[0], field[0], conductivity[0], wall_flags[0], leaf_solution[0, 0], parent
    )
    thin = (width, neumann.shape[1])
    other_neumann = from_partner(neumann, "box", 0)
    schur_two, inverse_two = local(
        second_map_kernel, [square] * 2, 20 * cube, parent, other_parent
    )
    inner_data, outer_data = local(
        data_kernel, [thin] * 2, 6 * cube, dtn_map, other_map, neumann, other_neumann, schur, inverse
    )
    other_inner = from_partner(inner_data, "box", 1)
    interface, own_side = local(
        second_data_kernel,
        [thin] * 2,
        4 * cube,
        inner_data,
        other_inner,
        schur_two,
        inverse_two,
        outward,
        outer_data,
    )
    other_side = from_partner(own_side, "box", 1)
    left = lax.axis_index("box") >> 1 & 1 == 0
    first = jnp.where(left, own_side, other_side)
    second = jnp.where(left, other_side, own_side)
    return (interface[None, None], jnp.concatenate([first, second], axis=0)[None, None])


def solution(mesh):
    return jax.shard_map(
        on_device,
        mesh=mesh,
        in_specs=(
            P("box", None, None, None, "slab", None),
            P("box", None, None, None, "slab"),
            P("box", None, None, "slab"),
            P("box", None, None, "slab"),
            P("box", "slab", None, None),
            P("box", "slab", None, None),
        ),
        out_specs=(P("box", "slab", None, None), P("box", "slab", None, None)),
        check_vma=False,
    )
```
